256 devices in a mesh: ctx: 64 (over z, x, core), head: 4 (over y).
Axes of the slice: x: 4, y: 4, z: 8, core: 2. Of those that a mesh axis runs over, the one named last changes fastest.
Arguments:
- queries: bfloat16 [8192, 4096], P('ctx', 'head'), may hold values from -40 to 40
- keys: bfloat16 [8192, 4096], P('ctx', 'head'), may hold values from -40 to 40
- values: bfloat16 [8192, 4096], P('ctx', 'head'), may hold values from -50 to 50
- pattern: int32 [64, 8], replicated, may hold values from -1 to 63, as said below
- upstream: bfloat16 [8192, 4096], P('ctx', 'head'), may hold values from -6 to 6
Outputs:
- normed: bfloat16 [8192, 4096], P('ctx', 'head')
- grad_queries: bfloat16 [8192, 4096], P('ctx', 'head')
- grad_keys: bfloat16 [8192, 4096], P('ctx', 'head')
- grad_values: bfloat16 [8192, 4096], P('ctx', 'head')
The draws below stay inside these ranges and needn't reach their ends.
Inputs may be any that keep to these rules, and one draw needn't show every extreme that they name: `pattern`: entry [i, k] for k < 7 is either i - 2^k or -1, and always -1 where i < 2^k; entry [i, 7] is i.
All inputs are finite; a program needn't handle non-finite values.
Results may differ from the reference program's by a relative error of at most 0.04.
Values may be sent and summed in bfloat16 or wider, within the bound.
A program may use at most 64 MiB of HBM per device.

```python
import jax
import jax.numpy as jnp
from jax import lax

HEADS = 32
HD = 128
BLOCK = 128
LEVELS = 7
TOKENS = 8192
WIDTH = 4096


def base_field(key):
    return jnp.clip(jax.random.normal(key, (TOKENS, HEADS * HD), jnp.float32), -4.0, 4.0)


def draw_queries(key, part):
    field = base_field(jax.random.fold_in(key, 1))
    return field.astype(jnp.bfloat16)


def draw_keys(key, part):
    field = base_field(jax.random.fold_in(key, 2))
    return field.astype(jnp.bfloat16)


def draw_values(key, part):
    field = base_field(jax.random.fold_in(key, 3))
    head_ids = (jnp.arange(HEADS * HD)[None, :] // HD).astype(jnp.float32)
    rising = head_ids / (HEADS - 1)
    head_scale = 3.0 ** rising
    row_scale = jnp.exp(jax.random.uniform(jax.random.fold_in(key, 4), (TOKENS, 1), jnp.float32, 0.0, 1.0986))
    return (field * head_scale * row_scale).astype(jnp.bfloat16)


def draw_pattern(key, part):
    blocks_all = TOKENS // BLOCK
    block_rows = jnp.arange(blocks_all, dtype=jnp.int32)[:, None]
    distances = (2 ** jnp.arange(LEVELS, dtype=jnp.int32))[None, :]
    kept_bits = jax.random.randint(key, (blocks_all, LEVELS), 0, 4) > 0
    target = block_rows - distances
    entries = jnp.where(kept_bits & (target >= 0), target, -1)
    return jnp.concatenate([entries, block_rows], axis=1).astype(jnp.int32)


def steps_of(own_key, dims, split, least, largest):
    loudness, own = 1.0, jax.random.fold_in(own_key, 6)
    for axis_at, blocks in split:
        steps = jnp.exp(jax.random.uniform(jax.random.fold_in(own, axis_at), (blocks,), jnp.float32, least / len(split), largest / len(split)))
        loudness = loudness * jnp.repeat(steps, dims[axis_at] // blocks).reshape([-1 if axis == axis_at else 1 for axis in range(len(dims))])
    return loudness


def normal_values(stream_key, dims, width, limit, split=(), held_as=jnp.bfloat16):
    array = width * jax.random.normal(stream_key, dims, jnp.float32)
    if split:
        array = array * steps_of(stream_key, dims, split, -0.22, 0.18)
    return jnp.clip(array, -limit, limit).astype(held_as)


def setup_inputs(seed: int = 0) -> dict:
    arg_keys = jax.random.split(jax.random.key(seed), 6)
    return {
        "queries": draw_queries(jax.random.fold_in(arg_keys[5], 71), 0),
        "keys": draw_keys(jax.random.fold_in(arg_keys[5], 71), 0),
        "values": draw_values(jax.random.fold_in(arg_keys[5], 71), 0),
        "pattern": draw_pattern(jax.random.fold_in(arg_keys[5], 71), 0),
        "upstream": normal_values(arg_keys[4], (TOKENS, WIDTH), 1.0, 6.0, ((0, 64), (1, 4))),
    }


NEG_BIG = -1e+30
EPSILON = 1e-06

def reference(queries, keys, values, pattern, upstream):
    block_count = TOKENS // BLOCK
    slot_count = LEVELS + 1
    score_scale = HD ** (-0.5)
    shape_blocks = (block_count, BLOCK, HEADS, HD)
    query_blocks = queries.reshape(shape_blocks)
    key_blocks = keys.reshape(shape_blocks)
    value_blocks = values.reshape(shape_blocks)
    positions = jnp.arange(BLOCK)
    causal = positions[None, :] <= positions[:, None]
    self_slot = jnp.arange(slot_count) == LEVELS

    def tiles_of(block_index):
        entries = pattern[block_index]
        live_slots = entries >= 0
        safe_index = jnp.maximum(entries, 0)
        keep_mask = live_slots[:, None, None] & (jnp.logical_not(self_slot)[:, None, None] | causal[None])
        return (safe_index, keep_mask)

    def scores_of(block_index, safe_index, keep_mask):
        key_tiles = key_blocks[safe_index].astype(jnp.float32)
        scores = jnp.einsum('qhd,skhd->hqsk', query_blocks[block_index].astype(jnp.float32), key_tiles) * score_scale
        return jnp.where(jnp.transpose(keep_mask, (1, 0, 2))[None], scores, NEG_BIG)

    def forward_block(block_index):
        safe_index, keep_mask = tiles_of(block_index)
        scores = scores_of(block_index, safe_index, keep_mask)
        highest = lax.optimization_barrier(jnp.max(scores, axis=(2, 3)))
        log_total = highest + jnp.log(lax.optimization_barrier(jnp.sum(jnp.exp(scores - highest[:, :, None, None]), axis=(2, 3))))
        prob_tiles = jnp.exp(scores - log_total[:, :, None, None]).astype(jnp.bfloat16)
        attention = jnp.einsum('hqsk,skhd->qhd', prob_tiles.astype(jnp.float32), value_blocks[safe_index].astype(jnp.float32))
        return (attention.astype(jnp.bfloat16), log_total)
    attention, log_total = lax.map(forward_block, jnp.arange(block_count))
    attn_wide = attention.reshape(TOKENS, WIDTH).astype(jnp.float32)
    square_sum = lax.optimization_barrier(jnp.sum(attn_wide * attn_wide, axis=1))
    inverse = lax.rsqrt(square_sum / WIDTH + EPSILON)
    normed = (attn_wide * inverse[:, None]).astype(jnp.bfloat16)
    upstream_wide = upstream.astype(jnp.float32)
    cross_term = lax.optimization_barrier(jnp.sum(upstream_wide * attn_wide, axis=1))
    grad_attn = (inverse[:, None] * upstream_wide - attn_wide * (inverse ** 3 * cross_term / WIDTH)[:, None]).astype(jnp.bfloat16)
    row_delta = lax.optimization_barrier(jnp.sum((grad_attn.astype(jnp.float32) * attn_wide).reshape(TOKENS, HEADS, HD), axis=2))
    row_delta = jnp.transpose(row_delta.reshape(block_count, BLOCK, HEADS), (0, 2, 1))
    grad_blocks = grad_attn.reshape(shape_blocks)

    def backward_block(accumulated, block_index):
        key_sum, value_sum = accumulated
        safe_index, keep_mask = tiles_of(block_index)
        scores = scores_of(block_index, safe_index, keep_mask)
        weights = jnp.exp(scores - log_total[block_index][:, :, None, None])
        prob_tiles = weights.astype(jnp.bfloat16)
        grad_here = grad_blocks[block_index].astype(jnp.float32)
        grad_probs = jnp.einsum('qhd,skhd->hqsk', grad_here, value_blocks[safe_index].astype(jnp.float32))
        dscore = (weights * (grad_probs - row_delta[block_index][:, :, None, None]) * score_scale).astype(jnp.bfloat16)
        dscore_wide = dscore.astype(jnp.float32)
        grad_query = jnp.einsum('hqsk,skhd->qhd', dscore_wide, key_blocks[safe_index].astype(jnp.float32))
        key_part = jnp.einsum('hqsk,qhd->skhd', dscore_wide, query_blocks[block_index].astype(jnp.float32))
        value_part = jnp.einsum('hqsk,qhd->skhd', prob_tiles.astype(jnp.float32), grad_here)
        key_sum = key_sum.at[safe_index].add(key_part)
        value_sum = value_sum.at[safe_index].add(value_part)
        return ((key_sum, value_sum), grad_query.astype(jnp.bfloat16))
    zeros_init = jnp.zeros(shape_blocks, jnp.float32)
    (key_sum, value_sum), grad_query = lax.scan(backward_block, (zeros_init, zeros_init), jnp.arange(block_count))
    grad_queries = grad_query.reshape(TOKENS, WIDTH)
    grad_keys = key_sum.astype(jnp.bfloat16).reshape(TOKENS, WIDTH)
    grad_values = value_sum.astype(jnp.bfloat16).reshape(TOKENS, WIDTH)
    return (normed, grad_queries, grad_keys, grad_values)
```

```python
import functools
import math

import jax
import jax.numpy as jnp
from jax import lax
from jax.experimental import pallas as pl
from jax.experimental.pallas import tpu as pltpu
from jax.sharding import PartitionSpec as P

HD = 128
BLOCK = 128
WIDTH = 4096
HEADS = 8
SLOTS = 7
OWN = 6
BLOCKS = 64
CHUNKS = 4
PER = HEADS // CHUNKS
NEG_BIG = -1e30
EPSILON = 1e-06
SCALE = HD**-0.5
SCALE2 = SCALE * math.log2(math.e)
MESH = pl.DeviceIdType.MESH
F32 = jnp.float32
BF16 = jnp.bfloat16


def nt(a, b):
    return lax.dot_general(a, b, (((1,), (1,)), ((), ())), preferred_element_type=F32)


def nn(a, b):
    return lax.dot_general(a, b, (((1,), (0,)), ((), ())), preferred_element_type=F32)


class Flow:
    def __init__(self, buf, send_sem, recv_sem, place, head, mirrored):
        self.buf, self.send_sem, self.recv_sem = buf, send_sem, recv_sem
        self.mirrored, self.head = mirrored, head
        self.j = BLOCKS - 1 - place if mirrored else place
        self.z, self.x, self.c = self.j // 8, (self.j // 2) % 4, self.j % 2

    def to(self, z, x, c):
        index = z * 8 + x * 2 + c
        index = BLOCKS - 1 - index if self.mirrored else index
        return (lax.rem(index + BLOCKS, BLOCKS), self.head)

    def copy(self, g, source, k, target=None):
        rows = pl.ds(g * PER, PER)
        return pltpu.make_async_remote_copy(
            src_ref=self.buf.at[rows, source],
            dst_ref=self.buf.at[rows, k],
            send_sem=self.send_sem.at[g, k],
            recv_sem=self.recv_sem.at[g, k],
            device_id=target or self.to(self.z, self.x, 1 - self.c),
            device_id_type=MESH,
        )

    def send(self, condition, g, source, k, z, x, c):
        @pl.when(condition)
        def _():
            self.copy(g, source, k, self.to(z, x, c)).start()

    def own(self, g):
        z, x, c = self.z, self.x, self.c
        self.send(z < 7, g, OWN, 3, z + 1, x, c)
        self.send((z == 1) | (z == 3), g, OWN, 5, z + 4, x, c)
        self.send(x < 3, g, OWN, 1, z, x + 1, c)
        self.send(x < 2, g, OWN, 2, z, x + 2, c)
        self.send(c == 0, g, OWN, 0, z, x, 1)

    def stage_a(self, g):
        z, x, c = self.z, self.x, self.c

        @pl.when(z >= 1)
        def _():
            self.copy(g, OWN, 3).wait_recv()
            self.send(z < 7, g, 3, 4, z + 1, x, c)
            self.send(x == 3, g, 3, 1, z, 0, c)
            self.send(x >= 2, g, 3, 2, z, x - 2, c)

    def stage_b(self, g):
        z, x, c = self.z, self.x, self.c

        @pl.when(z >= 2)
        def _():
            self.copy(g, OWN, 4).wait_recv()
            self.send((z == 2) | (z == 4), g, 4, 5, z + 2, x, c)

        @pl.when(self.j >= 2)
        def _():
            self.copy(g, OWN, 1).wait_recv()
            self.send(c == 1, g, 1, 0, z, x, 0)

    def stage_c(self, g):
        for condition, k in ((self.j >= 1, 0), (self.j >= 4, 2), (self.z >= 4, 5)):

            @pl.when(condition)
            def _():
                self.copy(g, OWN, k).wait_recv()

    def drain(self, g):
        z, x, c, j = self.z, self.x, self.c, self.j
        for condition, k in (
            ((c == 0) | (j >= 2), 0),
            ((x < 3) | (z >= 1), 1),
            ((x < 2) | (z >= 1), 2),
            (z < 7, 3),
            ((z >= 1) & (z < 7), 4),
            ((z >= 1) & (z <= 4), 5),
        ):

            @pl.when(condition)
            def _():
                self.copy(g, OWN, k).wait_send()

    def clear(self):
        for k in range(6):

            @pl.when(self.j < 2**k)
            def _():
                self.buf[:, k] = jnp.zeros(self.buf.shape[:1] + self.buf.shape[2:], self.buf.dtype)


def kernel(
    q_ref,
    k_ref,
    v_ref,
    pattern_ref,
    u_ref,
    normed_ref,
    dq_ref,
    dk_ref,
    dv_ref,
    kv,
    qs,
    gs,
    up,
    attn,
    probs,
    probs_t,
    row_scale,
    delta,
    stat_tile,
    stats,
    squares,
    crosses,
    y_buf,
    load_sem,
    kv_send,
    kv_recv,
    q_send,
    q_recv,
    g_send,
    g_recv,
    stat_send,
    stat_recv,
    y_send,
    y_recv,
):
    place = lax.axis_index("ctx")
    head = lax.axis_index("head")
    heads = lax.axis_size("head")
    z, x, c = place // 8, (place // 2) % 4, place % 2

    loads = []
    for h in range(HEADS):
        columns = pl.ds(h * HD, HD)
        for a, (ref, target) in enumerate(
            (
                (k_ref, kv.at[h, OWN, 0]),
                (v_ref, kv.at[h, OWN, 1]),
                (q_ref, qs.at[h, OWN]),
                (u_ref, up.at[h]),
            )
        ):
            copy = pltpu.make_async_copy(ref.at[:, columns], target, load_sem.at[a, h])
            copy.start()
            loads.append(copy)

    barrier = pltpu.get_barrier_semaphore()

    def ring(dz, dx, dc):
        return ((z + dz) % 8) * 8 + ((x + dx) % 4) * 2 + (c + dc) % 2

    partners = [(ring(d, 0, 0), head) for d in (1, 2, 4, 6, 7)]
    partners += [(ring(0, d, 0), head) for d in (1, 2, 3)]
    partners += [(ring(0, 0, 1), head)]
    partners += [((place + d) % BLOCKS, head) for d in (1, 2, 4, 60, 62, 63)]
    partners += [(place, (head + d) % heads) for d in range(1, heads)]
    for partner in partners:
        pl.semaphore_signal(barrier, inc=1, device_id=partner, device_id_type=MESH)

    kv_flow = Flow(kv, kv_send, kv_recv, place, head, False)
    q_flow = Flow(qs, q_send, q_recv, place, head, True)
    g_flow = Flow(gs, g_send, g_recv, place, head, True)
    for flow in (kv_flow, q_flow, g_flow):
        flow.clear()
    for k in range(6):

        @pl.when(g_flow.j < 2**k)
        def _():
            stats[k] = jnp.zeros(stats.shape[1:], F32)

    squares[...] = jnp.zeros(squares.shape, F32)
    crosses[...] = jnp.zeros(crosses.shape, F32)
    stat_tile[...] = jnp.zeros(stat_tile.shape, F32)
    for copy in loads:
        copy.wait()
    pl.semaphore_wait(barrier, len(partners))

    def every(body, count=CHUNKS):
        def step(g, carry):
            body(g)
            return carry

        lax.fori_loop(0, count, step, 0)

    every(kv_flow.own)
    every(q_flow.own)

    row = lax.broadcasted_iota(jnp.int32, (BLOCK, BLOCK), 0)
    lane = lax.broadcasted_iota(jnp.int32, (BLOCK, BLOCK), 1)

    def bias_of(index, k):
        return jnp.where(pattern_ref[index, k] >= 0, 0.0, NEG_BIG).astype(F32)

    def slot(array, s):
        return array[:, s * BLOCK : (s + 1) * BLOCK]

    def put(ref, h, value):
        ref[:, pl.ds(pl.multiple_of(h * HD, HD), HD)] = value

    def forward(h):
        raw = nt(qs[h, OWN], kv[h, :, 0].reshape(SLOTS * BLOCK, HD))
        scores = [slot(raw, s) * SCALE2 + bias_of(place, s) for s in range(OWN)]
        scores.append(jnp.where(lane <= row, slot(raw, OWN) * SCALE2, NEG_BIG))
        highest = jnp.max(functools.reduce(jnp.maximum, scores), axis=1, keepdims=True)
        weights = [jnp.exp2(s - highest) for s in scores]
        total = jnp.sum(functools.reduce(jnp.add, weights), axis=1, keepdims=True)
        inverse_total = 1.0 / total
        rounded = jnp.concatenate([w.astype(BF16) for w in weights], axis=1)
        probs[h] = rounded
        out = nn(rounded, kv[h, :, 1].reshape(SLOTS * BLOCK, HD)) * inverse_total
        out = out.astype(BF16)
        attn[h] = out
        wide = out.astype(F32)
        squares[...] += wide * wide
        crosses[...] += wide * up[h].astype(F32)
        row_scale[h] = inverse_total * SCALE
        stat_tile[...] = jnp.where(lane == h, highest + jnp.log2(total), stat_tile[...])

    def heads_of(g, body):
        def step(i, carry):
            body(g * PER + i)
            return carry

        lax.fori_loop(0, PER, step, 0)

    def first_phase(s):
        @pl.when(s < CHUNKS)
        def _():
            kv_flow.stage_a(s)

        @pl.when((s >= 1) & (s <= CHUNKS))
        def _():
            kv_flow.stage_b(s - 1)
            q_flow.stage_a(s - 1)

        @pl.when(s >= 2)
        def _():
            q_flow.stage_b(s - 2)
            kv_flow.stage_c(s - 2)
            heads_of(s - 2, forward)

    every(first_phase, CHUNKS + 2)

    square = jnp.sum(squares[...], axis=1, keepdims=True)
    cross = jnp.sum(crosses[...], axis=1, keepdims=True)
    tile = jnp.where(lane == 0, square, jnp.where(lane == 1, cross, 0.0))
    y_buf[heads - 1] = tile.T[:8]
    copies = []
    for d in range(1, heads):
        copy = pltpu.make_async_remote_copy(
            src_ref=y_buf.at[heads - 1],
            dst_ref=y_buf.at[d - 1],
            send_sem=y_send.at[d - 1],
            recv_sem=y_recv.at[d - 1],
            device_id=(place, (head + d) % heads),
            device_id_type=MESH,
        )
        copy.start()
        copies.append(copy)
    for copy in copies:
        copy.wait_recv()
    sums = functools.reduce(jnp.add, [y_buf[d] for d in range(heads)])
    sums = jnp.concatenate([sums, jnp.zeros((BLOCK - 8, BLOCK), F32)], axis=0).T
    inverse = lax.rsqrt(sums[:, 0:1] / WIDTH + EPSILON)
    factor = inverse * inverse * inverse * sums[:, 1:2] / WIDTH

    def gradient(h):
        wide = attn[h].astype(F32)
        grad = (inverse * up[h].astype(F32) - wide * factor).astype(BF16)
        gs[h, OWN] = grad
        put(normed_ref, h, (wide * inverse).astype(BF16))
        here = jnp.sum(grad.astype(F32) * wide, axis=1, keepdims=True)
        delta[h] = here
        stat_tile[...] = jnp.where(lane == h + HEADS, here, stat_tile[...])

    def gradient_chunk(g):
        heads_of(g, gradient)
        g_flow.own(g)

    every(gradient_chunk)

    stats[OWN] = stat_tile[...].T[: 2 * HEADS]

    def stat_copy(k):
        return pltpu.make_async_remote_copy(
            src_ref=stats.at[OWN],
            dst_ref=stats.at[k],
            send_sem=stat_send.at[k],
            recv_sem=stat_recv.at[k],
            device_id=(lax.rem(place - 2**k + BLOCKS, BLOCKS), head),
            device_id_type=MESH,
        )

    for k in range(6):

        @pl.when(place >= 2**k)
        def _():
            stat_copy(k).start()

    def grad_query(h):
        grad_probs = nt(gs[h, OWN], kv[h, :, 1].reshape(SLOTS * BLOCK, HD))
        held = probs[h].astype(F32)
        dscore = (held * (grad_probs - delta[h]) * row_scale[h]).astype(BF16)
        put(dq_ref, h, nn(dscore, kv[h, :, 0].reshape(SLOTS * BLOCK, HD)).astype(BF16))

    def key_probs(h):
        raw = nt(kv[h, OWN, 0], qs[h].reshape(SLOTS * BLOCK, HD))
        parts = []
        for s in range(SLOTS):
            scores = slot(raw, s) * SCALE2 - stats[s, pl.ds(h, 1), :]
            if s == OWN:
                scores = jnp.where(row <= lane, scores, NEG_BIG)
            else:
                index = place + 2**s
                live = (pattern_ref[jnp.minimum(index, BLOCKS - 1), s] >= 0) & (index < BLOCKS)
                scores = scores + jnp.where(live, 0.0, NEG_BIG).astype(F32)
            parts.append(jnp.exp2(scores).astype(BF16))
        probs_t[h] = jnp.concatenate(parts, axis=1)

    def grad_keys(h):
        grads = gs[h].reshape(SLOTS * BLOCK, HD)
        held = probs_t[h]
        put(dv_ref, h, nn(held, grads).astype(BF16))
        raw = nt(kv[h, OWN, 1], grads)
        parts = []
        for s in range(SLOTS):
            part = slot(raw, s) - stats[s, pl.ds(h + HEADS, 1), :]
            parts.append((slot(held, s).astype(F32) * part * SCALE).astype(BF16))
        dscore = jnp.concatenate(parts, axis=1)
        put(dk_ref, h, nn(dscore, qs[h].reshape(SLOTS * BLOCK, HD)).astype(BF16))

    def second_phase(s):
        @pl.when(s < CHUNKS)
        def _():
            heads_of(s, grad_query)
            g_flow.stage_a(s)

        @pl.when(s == 1)
        def _():
            for k in range(6):

                @pl.when(place + 2**k < BLOCKS)
                def _():
                    stat_copy(k).wait_recv()

        @pl.when((s >= 1) & (s <= CHUNKS))
        def _():
            g_flow.stage_b(s - 1)
            q_flow.stage_c(s - 1)
            heads_of(s - 1, key_probs)

        @pl.when(s >= 2)
        def _():
            g_flow.stage_c(s - 2)
            heads_of(s - 2, grad_keys)

    every(second_phase, CHUNKS + 2)

    every(kv_flow.drain)
    every(q_flow.drain)
    every(g_flow.drain)
    for copy in copies:
        copy.wait_send()
    for k in range(6):

        @pl.when(place >= 2**k)
        def _():
            stat_copy(k).wait_send()


def shards(queries, keys, values, pattern, upstream):
    heads = lax.axis_size("head")
    tokens, width = queries.shape
    out = jax.ShapeDtypeStruct((tokens, width), BF16)
    tile = (BLOCK, HD)
    dma = pltpu.SemaphoreType.DMA
    anywhere = pl.BlockSpec(memory_space=pl.ANY)
    return pl.pallas_call(
        kernel,
        out_shape=(out,) * 4,
        in_specs=[
            anywhere,
            anywhere,
            anywhere,
            pl.BlockSpec(memory_space=pltpu.SMEM),
            anywhere,
        ],
        out_specs=[pl.BlockSpec(memory_space=pltpu.VMEM)] * 4,
        scratch_shapes=[
            pltpu.VMEM((HEADS, SLOTS, 2) + tile, BF16),
            pltpu.VMEM((HEADS, SLOTS) + tile, BF16),
            pltpu.VMEM((HEADS, SLOTS) + tile, BF16),
            pltpu.VMEM((HEADS,) + tile, BF16),
            pltpu.VMEM((HEADS,) + tile, BF16),
            pltpu.VMEM((HEADS, BLOCK, SLOTS * BLOCK), BF16),
            pltpu.VMEM((HEADS, BLOCK, SLOTS * BLOCK), BF16),
            pltpu.VMEM((HEADS, BLOCK, 1), F32),
            pltpu.VMEM((HEADS, BLOCK, 1), F32),
            pltpu.VMEM((BLOCK, BLOCK), F32),
            pltpu.VMEM((SLOTS, 2 * HEADS, BLOCK), F32),
            pltpu.VMEM(tile, F32),
            pltpu.VMEM(tile, F32),
            pltpu.VMEM((heads, 8, BLOCK), F32),
            dma((4, HEADS)),
            dma((CHUNKS, 6)),
            dma((CHUNKS, 6)),
            dma((CHUNKS, 6)),
            dma((CHUNKS, 6)),
            dma((CHUNKS, 6)),
            dma((CHUNKS, 6)),
            dma((6,)),
            dma((6,)),
            dma((heads - 1,)),
            dma((heads - 1,)),
        ],
        compiler_params=pltpu.CompilerParams(
            collective_id=0, has_side_effects=True, vmem_limit_bytes=48 * 1024 * 1024
        ),
        cost_estimate=pl.CostEstimate(
            flops=2_000_000_000, bytes_accessed=2 * 1024 * 1024, transcendentals=2_000_000
        ),
    )(queries, keys, values, pattern, upstream)


def solution(mesh):
    return jax.shard_map(
        shards,
        mesh=mesh,
        in_specs=(P("ctx", "head"), P("ctx", "head"), P("ctx", "head"), P(), P("ctx", "head")),
        out_specs=(P("ctx", "head"), P("ctx", "head"), P("ctx", "head"), P("ctx", "head")),
        check_vma=False,
    )
```

```python
import functools
import math

import jax
import jax.numpy as jnp
from jax import lax
from jax.experimental import pallas as pl
from jax.experimental.pallas import tpu as pltpu
from jax.sharding import PartitionSpec as P

HD = 128
BLOCK = 128
WIDTH = 4096
HEADS = 8
SLOTS = 7
OWN = 6
LEVELS = 7
BLOCKS = 64
CHUNKS = 4
VMEM = 63 * 1024 * 1024
PER = HEADS // CHUNKS
LEAD = 1
NEG_BIG = -1e30
EPSILON = 1e-06
SCALE = HD**-0.5
SCALE2 = SCALE * math.log2(math.e)
MESH = pl.DeviceIdType.MESH
F32 = jnp.float32
BF16 = jnp.bfloat16


def nt(a, b):
    return lax.dot_general(a, b, (((1,), (1,)), ((), ())), preferred_element_type=F32)


def nn(a, b):
    return lax.dot_general(a, b, (((1,), (0,)), ((), ())), preferred_element_type=F32)


class Flow:
    def __init__(self, buf, send_sem, recv_sem, place, head, mirrored):
        self.buf, self.send_sem, self.recv_sem = buf, send_sem, recv_sem
        self.mirrored, self.head = mirrored, head
        self.j = BLOCKS - 1 - place if mirrored else place
        self.z, self.x, self.c = self.j // 8, (self.j // 2) % 4, self.j % 2

    def to(self, z, x, c):
        index = z * 8 + x * 2 + c
        index = BLOCKS - 1 - index if self.mirrored else index
        return (lax.rem(index + BLOCKS, BLOCKS), self.head)

    def copy(self, g, source, k, target=None):
        rows = pl.ds(g * PER, PER)
        return pltpu.make_async_remote_copy(
            src_ref=self.buf.at[rows, source],
            dst_ref=self.buf.at[rows, k],
            send_sem=self.send_sem.at[g, k],
            recv_sem=self.recv_sem.at[g, k],
            device_id=target or self.to(self.z, self.x, 1 - self.c),
            device_id_type=MESH,
        )

    def send(self, condition, g, source, k, z, x, c):
        @pl.when(condition)
        def _():
            self.copy(g, source, k, self.to(z, x, c)).start()

    def own(self, g):
        z, x, c = self.z, self.x, self.c
        self.send(z < 7, g, OWN, 3, z + 1, x, c)
        self.send(x < 3, g, OWN, 1, z, x + 1, c)
        self.send(x < 2, g, OWN, 2, z, x + 2, c)
        self.send(c == 0, g, OWN, 0, z, x, 1)

    def far(self, g):
        z, x, c = self.z, self.x, self.c
        self.send((z == 1) | (z == 3), g, OWN, 5, z + 4, x, c)

    def stage_a(self, g):
        z, x, c = self.z, self.x, self.c

        @pl.when(z >= 1)
        def _():
            self.copy(g, OWN, 3).wait_recv()
            self.send(z < 7, g, 3, 4, z + 1, x, c)
            self.send(x == 3, g, 3, 1, z, 0, c)
            self.send(x >= 2, g, 3, 2, z, x - 2, c)

    def stage_b(self, g):
        z, x, c = self.z, self.x, self.c

        @pl.when(z >= 2)
        def _():
            self.copy(g, OWN, 4).wait_recv()
            self.send((z == 2) | (z == 4), g, 4, 5, z + 2, x, c)

        @pl.when(self.j >= 2)
        def _():
            self.copy(g, OWN, 1).wait_recv()
            self.send(c == 1, g, 1, 0, z, x, 0)

    def stage_c(self, g):
        for condition, k in ((self.j >= 1, 0), (self.j >= 4, 2), (self.z >= 4, 5)):

            @pl.when(condition)
            def _():
                self.copy(g, OWN, k).wait_recv()

    def drain(self, g):
        z, x, c, j = self.z, self.x, self.c, self.j
        for condition, k in (
            ((c == 0) | (j >= 2), 0),
            ((x < 3) | (z >= 1), 1),
            ((x < 2) | (z >= 1), 2),
            (z < 7, 3),
            ((z >= 1) & (z < 7), 4),
            ((z >= 1) & (z <= 4), 5),
        ):

            @pl.when(condition)
            def _():
                self.copy(g, OWN, k).wait_send()

    def clear(self):
        for k in range(6):

            @pl.when(self.j < 2**k)
            def _():
                self.buf[:, k] = jnp.zeros(self.buf.shape[:1] + self.buf.shape[2:], self.buf.dtype)


def kernel(
    q_ref,
    k_ref,
    v_ref,
    pattern_hbm,
    u_ref,
    normed_ref,
    dq_ref,
    dk_ref,
    dv_ref,
    pattern_ref,
    staged,
    kv,
    qs,
    gs,
    up,
    attn,
    probs,
    probs_t,
    row_scale,
    delta,
    stat_tile,
    stats,
    squares,
    crosses,
    y_buf,
    pattern_sem,
    load_sem,
    store_sem,
    kv_send,
    kv_recv,
    q_send,
    q_recv,
    g_send,
    g_recv,
    stat_send,
    stat_recv,
    y_send,
    y_recv,
):
    place = lax.axis_index("ctx")
    head = lax.axis_index("head")
    heads = lax.axis_size("head")
    z, x, c = place // 8, (place // 2) % 4, place % 2

    barrier = pltpu.get_barrier_semaphore()

    def ring(dz, dx, dc):
        return ((z + dz) % 8) * 8 + ((x + dx) % 4) * 2 + (c + dc) % 2

    partners = [(ring(d, 0, 0), head) for d in (1, 2, 4, 6, 7)]
    partners += [(ring(0, d, 0), head) for d in (1, 2, 3)]
    partners += [(ring(0, 0, 1), head)]
    partners += [((place + d) % BLOCKS, head) for d in (1, 2, 4, 60, 62, 63)]
    partners += [(place, (head + d) % heads) for d in range(1, heads)]
    for partner in partners:
        pl.semaphore_signal(barrier, inc=1, device_id=partner, device_id_type=MESH)

    loads = [pltpu.make_async_copy(pattern_hbm, pattern_ref, pattern_sem)]
    for h in range(HEADS):
        columns = pl.ds(h * HD, HD)
        for a, (ref, target) in enumerate(
            (
                (k_ref, kv.at[h, OWN, 0]),
                (v_ref, kv.at[h, OWN, 1]),
                (q_ref, qs.at[h, OWN]),
                (u_ref, up.at[h]),
            )
        ):
            copy = pltpu.make_async_copy(ref.at[:, columns], target, load_sem.at[a, h])
            loads.append(copy)
    for copy in loads:
        copy.start()

    kv_flow = Flow(kv, kv_send, kv_recv, place, head, False)
    q_flow = Flow(qs, q_send, q_recv, place, head, True)
    g_flow = Flow(gs, g_send, g_recv, place, head, True)
    for flow in (kv_flow, q_flow, g_flow):
        flow.clear()
    for k in range(6):

        @pl.when(g_flow.j < 2**k)
        def _():
            stats[k] = jnp.zeros(stats.shape[1:], F32)

    squares[...] = jnp.zeros(squares.shape, F32)
    crosses[...] = jnp.zeros(crosses.shape, F32)
    stat_tile[...] = jnp.zeros(stat_tile.shape, F32)
    for copy in loads:
        copy.wait()
    pl.semaphore_wait(barrier, len(partners))

    def every(body, count=CHUNKS):
        def step(g, carry):
            body(g)
            return carry

        lax.fori_loop(0, count, step, 0)

    def kv_send_chunk(g):
        kv_flow.own(g)
        kv_flow.far(g)

    every(kv_send_chunk, LEAD)

    row = lax.broadcasted_iota(jnp.int32, (BLOCK, BLOCK), 0)
    lane = lax.broadcasted_iota(jnp.int32, (BLOCK, BLOCK), 1)

    def bias_of(index, k):
        return jnp.where(pattern_ref[k, index] >= 0, 0.0, NEG_BIG).astype(F32)

    def slot(array, s):
        return array[:, s * BLOCK : (s + 1) * BLOCK]

    results = (normed_ref, dq_ref, dk_ref, dv_ref)

    def store(a, h):
        columns = pl.ds(pl.multiple_of(h * HD, HD), HD)
        return pltpu.make_async_copy(
            staged.at[a, h], results[a].at[:, columns], store_sem.at[a, h]
        )

    def put(a, h, value):
        staged[a, h] = value
        store(a, h).start()

    def forward(h):
        raw = nt(qs[h, OWN], kv[h, :, 0].reshape(SLOTS * BLOCK, HD))
        scores = [slot(raw, s) * SCALE2 + bias_of(place, s) for s in range(OWN)]
        scores.append(jnp.where(lane <= row, slot(raw, OWN) * SCALE2, NEG_BIG))
        highest = jnp.max(functools.reduce(jnp.maximum, scores), axis=1, keepdims=True)
        weights = [jnp.exp2(s - highest) for s in scores]
        total = jnp.sum(functools.reduce(jnp.add, weights), axis=1, keepdims=True)
        inverse_total = 1.0 / total
        rounded = jnp.concatenate([w.astype(BF16) for w in weights], axis=1)
        probs[h] = rounded
        out = nn(rounded, kv[h, :, 1].reshape(SLOTS * BLOCK, HD)) * inverse_total
        out = out.astype(BF16)
        attn[h] = out
        wide = out.astype(F32)
        squares[...] += wide * wide
        crosses[...] += wide * up[h].astype(F32)
        row_scale[h] = inverse_total * SCALE
        stat_tile[...] = jnp.where(lane == h, highest + jnp.log2(total), stat_tile[...])

    def heads_of(g, body):
        def step(i, carry):
            body(g * PER + i)
            return carry

        lax.fori_loop(0, PER, step, 0)

    def first_phase(s):
        @pl.when(s < CHUNKS)
        def _():
            kv_flow.stage_a(s)

        @pl.when(s < CHUNKS - LEAD)
        def _():
            kv_send_chunk(s + LEAD)

        @pl.when((s >= 1) & (s <= CHUNKS))
        def _():
            kv_flow.stage_b(s - 1)

        @pl.when(s < CHUNKS)
        def _():
            q_flow.own(s)

        @pl.when(s >= 2)
        def _():
            q_flow.stage_a(s - 2)
            kv_flow.stage_c(s - 2)
            heads_of(s - 2, forward)

    every(first_phase, CHUNKS + 2)

    stats[OWN, 0] = stat_tile[...].T[:HEADS]

    def stat_copy(k, part):
        return pltpu.make_async_remote_copy(
            src_ref=stats.at[OWN, part],
            dst_ref=stats.at[k, part],
            send_sem=stat_send.at[k, part],
            recv_sem=stat_recv.at[k, part],
            device_id=(lax.rem(place - 2**k + BLOCKS, BLOCKS), head),
            device_id_type=MESH,
        )

    def stat_start(part):
        for k in range(6):

            @pl.when(place >= 2**k)
            def _():
                stat_copy(k, part).start()

    def stat_wait(part):
        for k in range(6):

            @pl.when(place + 2**k < BLOCKS)
            def _():
                stat_copy(k, part).wait_recv()

    square = jnp.sum(squares[...], axis=1, keepdims=True)
    cross = jnp.sum(crosses[...], axis=1, keepdims=True)
    tile = jnp.where(lane == 0, square, jnp.where(lane == 1, cross, 0.0))
    y_buf[heads - 1] = tile.T[:8]
    copies = []
    for d in range(1, heads):
        copy = pltpu.make_async_remote_copy(
            src_ref=y_buf.at[heads - 1],
            dst_ref=y_buf.at[d - 1],
            send_sem=y_send.at[d - 1],
            recv_sem=y_recv.at[d - 1],
            device_id=(place, (head + d) % heads),
            device_id_type=MESH,
        )
        copy.start()
        copies.append(copy)
    stat_start(0)

    def q_rest(g):
        q_flow.far(g)
        q_flow.stage_b(g)

    every(q_rest)
    for copy in copies:
        copy.wait_recv()
    sums = functools.reduce(jnp.add, [y_buf[d] for d in range(heads)])
    sums = jnp.concatenate([sums, jnp.zeros((BLOCK - 8, BLOCK), F32)], axis=0).T
    inverse = lax.rsqrt(sums[:, 0:1] / WIDTH + EPSILON)
    factor = inverse * inverse * inverse * sums[:, 1:2] / WIDTH

    def gradient(h):
        wide = attn[h].astype(F32)
        grad = (inverse * up[h].astype(F32) - wide * factor).astype(BF16)
        gs[h, OWN] = grad
        put(0, h, (wide * inverse).astype(BF16))
        here = jnp.sum(grad.astype(F32) * wide, axis=1, keepdims=True)
        delta[h] = here
        stat_tile[...] = jnp.where(lane == h, here, stat_tile[...])

    def gradient_chunk(g):
        heads_of(g, gradient)
        g_flow.own(g)
        g_flow.far(g)

    every(gradient_chunk)
    stats[OWN, 1] = stat_tile[...].T[:HEADS]
    stat_start(1)

    def grad_query(h):
        grad_probs = nt(gs[h, OWN], kv[h, :, 1].reshape(SLOTS * BLOCK, HD))
        held = probs[h].astype(F32)
        dscore = (held * (grad_probs - delta[h]) * row_scale[h]).astype(BF16)
        put(1, h, nn(dscore, kv[h, :, 0].reshape(SLOTS * BLOCK, HD)).astype(BF16))

    def key_probs(h):
        raw = nt(kv[h, OWN, 0], qs[h].reshape(SLOTS * BLOCK, HD))
        parts = []
        for s in range(SLOTS):
            scores = slot(raw, s) * SCALE2 - stats[s, 0, pl.ds(h, 1), :]
            if s == OWN:
                scores = jnp.where(row <= lane, scores, NEG_BIG)
            else:
                index = place + 2**s
                live = (pattern_ref[s, jnp.minimum(index, BLOCKS - 1)] >= 0) & (index < BLOCKS)
                scores = scores + jnp.where(live, 0.0, NEG_BIG).astype(F32)
            parts.append(jnp.exp2(scores).astype(BF16))
        probs_t[h] = jnp.concatenate(parts, axis=1)

    def grad_keys(h):
        grads = gs[h].reshape(SLOTS * BLOCK, HD)
        held = probs_t[h]
        put(3, h, nn(held, grads).astype(BF16))
        raw = nt(kv[h, OWN, 1], grads)
        parts = []
        for s in range(SLOTS):
            part = slot(raw, s) - stats[s, 1, pl.ds(h, 1), :]
            parts.append((slot(held, s).astype(F32) * part * SCALE).astype(BF16))
        dscore = jnp.concatenate(parts, axis=1)
        put(2, h, nn(dscore, qs[h].reshape(SLOTS * BLOCK, HD)).astype(BF16))

    def second_phase(s):
        @pl.when(s < CHUNKS)
        def _():
            heads_of(s, grad_query)
            g_flow.stage_a(s)

        @pl.when(s == 1)
        def _():
            stat_wait(0)

        @pl.when(s == 2)
        def _():
            stat_wait(1)

        @pl.when((s >= 1) & (s <= CHUNKS))
        def _():
            g_flow.stage_b(s - 1)
            q_flow.stage_c(s - 1)
            heads_of(s - 1, key_probs)

        @pl.when(s >= 2)
        def _():
            g_flow.stage_c(s - 2)
            heads_of(s - 2, grad_keys)

    every(second_phase, CHUNKS + 2)

    every(kv_flow.drain)
    every(q_flow.drain)
    every(g_flow.drain)
    for copy in copies:
        copy.wait_send()
    for k in range(6):

        @pl.when(place >= 2**k)
        def _():
            stat_copy(k, 0).wait_send()
            stat_copy(k, 1).wait_send()

    def stored(h):
        for a in range(4):
            store(a, h).wait()

    every(stored, HEADS)


def copy_kernel(*refs):
    sources, targets, held, sem = refs[:4], refs[4:8], refs[8], refs[9]
    halves = []
    for a in range(4):
        for part in range(2):
            rows = pl.ds(part * BLOCK // 2, BLOCK // 2)
            here = held.at[a, rows]
            halves.append(
                (
                    pltpu.make_async_copy(sources[a].at[rows], here, sem.at[0, a, part]),
                    pltpu.make_async_copy(here, targets[a].at[rows], sem.at[1, a, part]),
                )
            )
    for load, _ in halves:
        load.start()
    for load, store in halves:
        load.wait()
        store.start()
    for _, store in halves:
        store.wait()


def shards(queries, keys, values, pattern, upstream):
    heads = lax.axis_size("head")
    tokens, width = queries.shape
    out = jax.ShapeDtypeStruct((tokens, width), BF16)
    tile = (BLOCK, HD)
    dma = pltpu.SemaphoreType.DMA
    anywhere = pl.BlockSpec(memory_space=pl.ANY)
    results = pl.pallas_call(
        kernel,
        out_shape=(out,) * 4,
        in_specs=[
            anywhere,
            anywhere,
            anywhere,
            anywhere,
            anywhere,
        ],
        out_specs=[anywhere] * 4,
        scratch_shapes=[
            pltpu.SMEM((LEVELS + 1, BLOCKS), jnp.int32),
            pltpu.VMEM((4, HEADS) + tile, BF16),
            pltpu.VMEM((HEADS, SLOTS, 2) + tile, BF16),
            pltpu.VMEM((HEADS, SLOTS) + tile, BF16),
            pltpu.VMEM((HEADS, SLOTS) + tile, BF16),
            pltpu.VMEM((HEADS,) + tile, BF16),
            pltpu.VMEM((HEADS,) + tile, BF16),
            pltpu.VMEM((HEADS, BLOCK, SLOTS * BLOCK), BF16),
            pltpu.VMEM((HEADS, BLOCK, SLOTS * BLOCK), BF16),
            pltpu.VMEM((HEADS, BLOCK, 1), F32),
            pltpu.VMEM((HEADS, BLOCK, 1), F32),
            pltpu.VMEM((BLOCK, BLOCK), F32),
            pltpu.VMEM((SLOTS, 2, HEADS, BLOCK), F32),
            pltpu.VMEM(tile, F32),
            pltpu.VMEM(tile, F32),
            pltpu.VMEM((heads, 8, BLOCK), F32),
            dma,
            dma((4, HEADS)),
            dma((4, HEADS)),
            dma((CHUNKS, 6)),
            dma((CHUNKS, 6)),
            dma((CHUNKS, 6)),
            dma((CHUNKS, 6)),
            dma((CHUNKS, 6)),
            dma((CHUNKS, 6)),
            dma((6, 2)),
            dma((6, 2)),
            dma((heads - 1,)),
            dma((heads - 1,)),
        ],
        compiler_params=pltpu.CompilerParams(
            collective_id=0, has_side_effects=True, vmem_limit_bytes=VMEM
        ),
        cost_estimate=pl.CostEstimate(
            flops=2_000_000_000, bytes_accessed=2 * 1024 * 1024, transcendentals=2_000_000
        ),
    )(queries, keys, values, pattern.T, upstream)
    return pl.pallas_call(
        copy_kernel,
        out_shape=(out,) * 4,
        in_specs=[anywhere] * 4,
        out_specs=[anywhere] * 4,
        scratch_shapes=[pltpu.VMEM((4, tokens, width), BF16), dma((2, 4, 2))],
        compiler_params=pltpu.CompilerParams(vmem_limit_bytes=VMEM),
    )(*results)


def solution(mesh):
    return jax.shard_map(
        shards,
        mesh=mesh,
        in_specs=(P("ctx", "head"), P("ctx", "head"), P("ctx", "head"), P(), P("ctx", "head")),
        out_specs=(P("ctx", "head"), P("ctx", "head"), P("ctx", "head"), P("ctx", "head")),
        check_vma=False,
    )
```

```python
import functools
import math

import jax
import jax.numpy as jnp
from jax import lax
from jax.experimental import pallas as pl
from jax.experimental.pallas import tpu as pltpu
from jax.sharding import PartitionSpec as P

HD = 128
BLOCK = 128
WIDTH = 4096
HEADS = 8
SLOTS = 7
OWN = 6
LEVELS = 7
BLOCKS = 64
CHUNKS = 4
VMEM = 63 * 1024 * 1024
PER = HEADS // CHUNKS
LEAD = 1
LAG_B = 1
LAG_C = 2
LAG_QA = 1
LAG_QB = 2
G_LAG_P = 1
KV_RELAYED = 0
Q_RELAYED = 4
G_RELAYED = 0
G_LAG_B = 1
G_LAG_C = 2
NEG_BIG = -1e30
EPSILON = 1e-06
SCALE = HD**-0.5
SCALE2 = SCALE * math.log2(math.e)
MESH = pl.DeviceIdType.MESH
F32 = jnp.float32
BF16 = jnp.bfloat16


def nt(a, b):
    return lax.dot_general(a, b, (((1,), (1,)), ((), ())), preferred_element_type=F32)


def nn(a, b):
    return lax.dot_general(a, b, (((1,), (0,)), ((), ())), preferred_element_type=F32)


class Flow:
    def __init__(self, buf, send_sem, recv_sem, place, head, mirrored, relayed):
        self.buf, self.send_sem, self.recv_sem = buf, send_sem, recv_sem
        self.mirrored, self.head, self.relayed = mirrored, head, relayed
        self.j = BLOCKS - 1 - place if mirrored else place
        self.z, self.x, self.c = self.j // 8, (self.j // 2) % 4, self.j % 2

    def to(self, z, x, c):
        index = z * 8 + x * 2 + c
        index = BLOCKS - 1 - index if self.mirrored else index
        return (lax.rem(index + BLOCKS, BLOCKS), self.head)

    def copy(self, g, source, k, target=None):
        rows = pl.ds(g * PER, PER)
        return pltpu.make_async_remote_copy(
            src_ref=self.buf.at[rows, source],
            dst_ref=self.buf.at[rows, k],
            send_sem=self.send_sem.at[g, k],
            recv_sem=self.recv_sem.at[g, k],
            device_id=target or self.to(self.z, self.x, 1 - self.c),
            device_id_type=MESH,
        )

    def send(self, condition, g, source, k, z, x, c):
        @pl.when(condition)
        def _():
            self.copy(g, source, k, self.to(z, x, c)).start()

    def own(self, g):
        z, x, c = self.z, self.x, self.c
        self.send(z < 7, g, OWN, 3, z + 1, x, c)

    def own_x(self, g):
        z, x, c = self.z, self.x, self.c
        self.send(x < 3, g, OWN, 1, z, x + 1, c)
        self.send(x < 2, g, OWN, 2, z, x + 2, c)
        self.send(c == 0, g, OWN, 0, z, x, 1)

    def direct(self, g):
        return ((self.z == 1) | (self.z == 3)) & (g >= self.relayed)

    def relay(self, g):
        z = self.z
        return (z == 2) | (z == 4) | (((z == 3) | (z == 5)) & (g < self.relayed))

    def far(self, g):
        self.send(self.direct(g), g, OWN, 5, self.z + 4, self.x, self.c)

    def stage_a(self, g):
        z, x, c = self.z, self.x, self.c

        @pl.when(z >= 1)
        def _():
            self.copy(g, OWN, 3).wait_recv()
            self.send(z < 7, g, 3, 4, z + 1, x, c)
            self.send(x == 3, g, 3, 1, z, 0, c)
            self.send(x >= 2, g, 3, 2, z, x - 2, c)

    def stage_b(self, g):
        z, x, c = self.z, self.x, self.c

        @pl.when(z >= 2)
        def _():
            self.copy(g, OWN, 4).wait_recv()
            self.send(self.relay(g), g, 4, 5, z + 2, x, c)

        @pl.when(self.j >= 2)
        def _():
            self.copy(g, OWN, 1).wait_recv()
            self.send(c == 1, g, 1, 0, z, x, 0)

    def stage_c(self, g):
        for condition, k in ((self.j >= 1, 0), (self.j >= 4, 2), (self.z >= 4, 5)):

            @pl.when(condition)
            def _():
                self.copy(g, OWN, k).wait_recv()

    def drain(self, g):
        z, x, c, j = self.z, self.x, self.c, self.j
        for condition, k in (
            ((c == 0) | (j >= 2), 0),
            ((x < 3) | (z >= 1), 1),
            ((x < 2) | (z >= 1), 2),
            (z < 7, 3),
            ((z >= 1) & (z < 7), 4),
            (self.direct(g) | self.relay(g), 5),
        ):

            @pl.when(condition)
            def _():
                self.copy(g, OWN, k).wait_send()

    def clear(self):
        for k in range(6):

            @pl.when(self.j < 2**k)
            def _():
                self.buf[:, k] = jnp.zeros(self.buf.shape[:1] + self.buf.shape[2:], self.buf.dtype)


def kernel(
    q_ref,
    k_ref,
    v_ref,
    pattern_hbm,
    u_ref,
    normed_ref,
    dq_ref,
    dk_ref,
    dv_ref,
    pattern_ref,
    staged,
    kv,
    qs,
    gs,
    up,
    attn,
    probs,
    probs_t,
    row_scale,
    delta,
    stat_tile,
    stats,
    squares,
    crosses,
    y_buf,
    pattern_sem,
    load_sem,
    store_sem,
    kv_send,
    kv_recv,
    q_send,
    q_recv,
    g_send,
    g_recv,
    stat_send,
    stat_recv,
    y_send,
    y_recv,
):
    place = lax.axis_index("ctx")
    head = lax.axis_index("head")
    heads = lax.axis_size("head")
    z, x, c = place // 8, (place // 2) % 4, place % 2

    barrier = pltpu.get_barrier_semaphore()

    def ring(dz, dx, dc):
        return ((z + dz) % 8) * 8 + ((x + dx) % 4) * 2 + (c + dc) % 2

    partners = [(ring(d, 0, 0), head) for d in (1, 2, 4, 6, 7)]
    partners += [(ring(0, d, 0), head) for d in (1, 2, 3)]
    partners += [(ring(0, 0, 1), head)]
    partners += [((place + d) % BLOCKS, head) for d in (1, 2, 4, 60, 62, 63)]
    partners += [(place, (head + d) % heads) for d in range(1, heads)]
    for partner in partners:
        pl.semaphore_signal(barrier, inc=1, device_id=partner, device_id_type=MESH)

    loads = [pltpu.make_async_copy(pattern_hbm, pattern_ref, pattern_sem)]
    for h in range(HEADS):
        columns = pl.ds(h * HD, HD)
        for a, (ref, target) in enumerate(
            (
                (k_ref, kv.at[h, OWN, 0]),
                (v_ref, kv.at[h, OWN, 1]),
                (q_ref, qs.at[h, OWN]),
                (u_ref, up.at[h]),
            )
        ):
            copy = pltpu.make_async_copy(ref.at[:, columns], target, load_sem.at[a, h])
            loads.append(copy)
    for copy in loads:
        copy.start()

    kv_flow = Flow(kv, kv_send, kv_recv, place, head, False, KV_RELAYED)
    q_flow = Flow(qs, q_send, q_recv, place, head, True, Q_RELAYED)
    g_flow = Flow(gs, g_send, g_recv, place, head, True, G_RELAYED)
    for flow in (kv_flow, q_flow, g_flow):
        flow.clear()
    for k in range(6):

        @pl.when(g_flow.j < 2**k)
        def _():
            stats[k] = jnp.zeros(stats.shape[1:], F32)

    squares[...] = jnp.zeros(squares.shape, F32)
    crosses[...] = jnp.zeros(crosses.shape, F32)
    stat_tile[...] = jnp.zeros(stat_tile.shape, F32)
    for copy in loads:
        copy.wait()
    pl.semaphore_wait(barrier, len(partners))

    def every(body, count=CHUNKS):
        def step(g, carry):
            body(g)
            return carry

        lax.fori_loop(0, count, step, 0)

    def kv_send_chunk(g):
        kv_flow.own(g)
        kv_flow.far(g)

    every(kv_send_chunk, LEAD)

    row = lax.broadcasted_iota(jnp.int32, (BLOCK, BLOCK), 0)
    lane = lax.broadcasted_iota(jnp.int32, (BLOCK, BLOCK), 1)

    def bias_of(index, k):
        return jnp.where(pattern_ref[k, index] >= 0, 0.0, NEG_BIG).astype(F32)

    def slot(array, s):
        return array[:, s * BLOCK : (s + 1) * BLOCK]

    results = (normed_ref, dq_ref, dk_ref, dv_ref)

    def store(a, h):
        columns = pl.ds(pl.multiple_of(h * HD, HD), HD)
        return pltpu.make_async_copy(
            staged.at[a, h], results[a].at[:, columns], store_sem.at[a, h]
        )

    def put(a, h, value):
        staged[a, h] = value
        store(a, h).start()

    def forward(h):
        raw = nt(qs[h, OWN], kv[h, :, 0].reshape(SLOTS * BLOCK, HD))
        scores = [slot(raw, s) * SCALE2 + bias_of(place, s) for s in range(OWN)]
        scores.append(jnp.where(lane <= row, slot(raw, OWN) * SCALE2, NEG_BIG))
        highest = jnp.max(functools.reduce(jnp.maximum, scores), axis=1, keepdims=True)
        weights = [jnp.exp2(s - highest) for s in scores]
        total = jnp.sum(functools.reduce(jnp.add, weights), axis=1, keepdims=True)
        inverse_total = 1.0 / total
        rounded = jnp.concatenate([w.astype(BF16) for w in weights], axis=1)
        probs[h] = rounded
        out = nn(rounded, kv[h, :, 1].reshape(SLOTS * BLOCK, HD)) * inverse_total
        out = out.astype(BF16)
        attn[h] = out
        wide = out.astype(F32)
        squares[...] += wide * wide
        crosses[...] += wide * up[h].astype(F32)
        row_scale[h] = inverse_total * SCALE
        stat_tile[...] = jnp.where(lane == h, highest + jnp.log2(total), stat_tile[...])

    def heads_of(g, body):
        def step(i, carry):
            body(g * PER + i)
            return carry

        lax.fori_loop(0, PER, step, 0)

    def at(step, body):
        @pl.when((step >= 0) & (step < CHUNKS))
        def _():
            body(step)

    def kv_done(g):
        kv_flow.stage_c(g)
        heads_of(g, forward)

    def q_send_chunk(g):
        q_flow.own(g)
        q_flow.far(g)

    def first_phase(s):
        at(s, kv_flow.stage_a)

        @pl.when(s < CHUNKS - LEAD)
        def _():
            kv_send_chunk(s + LEAD)

        at(s, kv_flow.own_x)

        at(s - LAG_B, kv_flow.stage_b)
        at(s, q_send_chunk)
        at(s, q_flow.own_x)
        at(s - LAG_QA, q_flow.stage_a)
        at(s - LAG_QB, q_flow.stage_b)
        at(s - LAG_C, kv_done)

    every(first_phase, CHUNKS + max(LAG_C, LAG_QB))

    stats[OWN, 0] = stat_tile[...].T[:HEADS]

    def stat_copy(k, part):
        return pltpu.make_async_remote_copy(
            src_ref=stats.at[OWN, part],
            dst_ref=stats.at[k, part],
            send_sem=stat_send.at[k, part],
            recv_sem=stat_recv.at[k, part],
            device_id=(lax.rem(place - 2**k + BLOCKS, BLOCKS), head),
            device_id_type=MESH,
        )

    def stat_start(part):
        for k in range(6):

            @pl.when(place >= 2**k)
            def _():
                stat_copy(k, part).start()

    def stat_wait(part):
        for k in range(6):

            @pl.when(place + 2**k < BLOCKS)
            def _():
                stat_copy(k, part).wait_recv()

    square = jnp.sum(squares[...], axis=1, keepdims=True)
    cross = jnp.sum(crosses[...], axis=1, keepdims=True)
    tile = jnp.where(lane == 0, square, jnp.where(lane == 1, cross, 0.0))
    y_buf[heads - 1] = tile.T[:8]
    copies = []
    for d in range(1, heads):
        copy = pltpu.make_async_remote_copy(
            src_ref=y_buf.at[heads - 1],
            dst_ref=y_buf.at[d - 1],
            send_sem=y_send.at[d - 1],
            recv_sem=y_recv.at[d - 1],
            device_id=(place, (head + d) % heads),
            device_id_type=MESH,
        )
        copy.start()
        copies.append(copy)
    stat_start(0)

    for copy in copies:
        copy.wait_recv()
    sums = functools.reduce(jnp.add, [y_buf[d] for d in range(heads)])
    sums = jnp.concatenate([sums, jnp.zeros((BLOCK - 8, BLOCK), F32)], axis=0).T
    inverse = lax.rsqrt(sums[:, 0:1] / WIDTH + EPSILON)
    factor = inverse * inverse * inverse * sums[:, 1:2] / WIDTH

    def gradient(h):
        wide = attn[h].astype(F32)
        grad = (inverse * up[h].astype(F32) - wide * factor).astype(BF16)
        gs[h, OWN] = grad
        put(0, h, (wide * inverse).astype(BF16))
        here = jnp.sum(grad.astype(F32) * wide, axis=1, keepdims=True)
        delta[h] = here
        stat_tile[...] = jnp.where(lane == h, here, stat_tile[...])

    def g_send(g):
        g_flow.own(g)
        g_flow.own_x(g)
        g_flow.far(g)

    def gradient_chunk(g):
        heads_of(g, gradient)

    every(gradient_chunk)
    stats[OWN, 1] = stat_tile[...].T[:HEADS]
    stat_start(1)

    def grad_query(h):
        grad_probs = nt(gs[h, OWN], kv[h, :, 1].reshape(SLOTS * BLOCK, HD))
        held = probs[h].astype(F32)
        dscore = (held * (grad_probs - delta[h]) * row_scale[h]).astype(BF16)
        put(1, h, nn(dscore, kv[h, :, 0].reshape(SLOTS * BLOCK, HD)).astype(BF16))

    def key_probs(h):
        raw = nt(kv[h, OWN, 0], qs[h].reshape(SLOTS * BLOCK, HD))
        parts = []
        for s in range(SLOTS):
            scores = slot(raw, s) * SCALE2 - stats[s, 0, pl.ds(h, 1), :]
            if s == OWN:
                scores = jnp.where(row <= lane, scores, NEG_BIG)
            else:
                index = place + 2**s
                live = (pattern_ref[s, jnp.minimum(index, BLOCKS - 1)] >= 0) & (index < BLOCKS)
                scores = scores + jnp.where(live, 0.0, NEG_BIG).astype(F32)
            parts.append(jnp.exp2(scores).astype(BF16))
        probs_t[h] = jnp.concatenate(parts, axis=1)

    def grad_keys(h):
        grads = gs[h].reshape(SLOTS * BLOCK, HD)
        held = probs_t[h]
        put(3, h, nn(held, grads).astype(BF16))
        raw = nt(kv[h, OWN, 1], grads)
        parts = []
        for s in range(SLOTS):
            part = slot(raw, s) - stats[s, 1, pl.ds(h, 1), :]
            parts.append((slot(held, s).astype(F32) * part * SCALE).astype(BF16))
        dscore = jnp.concatenate(parts, axis=1)
        put(2, h, nn(dscore, qs[h].reshape(SLOTS * BLOCK, HD)).astype(BF16))

    every(g_send)

    def key_probs_chunk(g):
        @pl.when(g == 0)
        def _():
            stat_wait(0)

        q_flow.stage_c(g)
        heads_of(g, key_probs)

    def key_grads(g):
        @pl.when(g == 0)
        def _():
            stat_wait(1)

        g_flow.stage_c(g)
        heads_of(g, grad_keys)

    def grad_query_chunk(g):
        heads_of(g, grad_query)

    def second_phase(s):
        at(s, grad_query_chunk)
        at(s, g_flow.stage_a)
        at(s - G_LAG_B, g_flow.stage_b)
        at(s - G_LAG_P, key_probs_chunk)
        at(s - G_LAG_C, key_grads)

    every(second_phase, CHUNKS + G_LAG_C)

    every(kv_flow.drain)
    every(q_flow.drain)
    every(g_flow.drain)
    for copy in copies:
        copy.wait_send()
    for k in range(6):

        @pl.when(place >= 2**k)
        def _():
            stat_copy(k, 0).wait_send()
            stat_copy(k, 1).wait_send()

    def stored(h):
        for a in range(4):
            store(a, h).wait()

    every(stored, HEADS)


def copy_kernel(*refs):
    sources, targets, held, sem = refs[:4], refs[4:8], refs[8], refs[9]
    halves = []
    for a in range(4):
        for part in range(2):
            rows = pl.ds(part * BLOCK // 2, BLOCK // 2)
            here = held.at[a, rows]
            halves.append(
                (
                    pltpu.make_async_copy(sources[a].at[rows], here, sem.at[0, a, part]),
                    pltpu.make_async_copy(here, targets[a].at[rows], sem.at[1, a, part]),
                )
            )
    for load, _ in halves:
        load.start()
    for load, store in halves:
        load.wait()
        store.start()
    for _, store in halves:
        store.wait()


def shards(queries, keys, values, pattern, upstream):
    heads = lax.axis_size("head")
    tokens, width = queries.shape
    out = jax.ShapeDtypeStruct((tokens, width), BF16)
    tile = (BLOCK, HD)
    dma = pltpu.SemaphoreType.DMA
    anywhere = pl.BlockSpec(memory_space=pl.ANY)
    results = pl.pallas_call(
        kernel,
        out_shape=(out,) * 4,
        in_specs=[
            anywhere,
            anywhere,
            anywhere,
            anywhere,
            anywhere,
        ],
        out_specs=[anywhere] * 4,
        scratch_shapes=[
            pltpu.SMEM((LEVELS + 1, BLOCKS), jnp.int32),
            pltpu.VMEM((4, HEADS) + tile, BF16),
            pltpu.VMEM((HEADS, SLOTS, 2) + tile, BF16),
            pltpu.VMEM((HEADS, SLOTS) + tile, BF16),
            pltpu.VMEM((HEADS, SLOTS) + tile, BF16),
            pltpu.VMEM((HEADS,) + tile, BF16),
            pltpu.VMEM((HEADS,) + tile, BF16),
            pltpu.VMEM((HEADS, BLOCK, SLOTS * BLOCK), BF16),
            pltpu.VMEM((HEADS, BLOCK, SLOTS * BLOCK), BF16),
            pltpu.VMEM((HEADS, BLOCK, 1), F32),
            pltpu.VMEM((HEADS, BLOCK, 1), F32),
            pltpu.VMEM((BLOCK, BLOCK), F32),
            pltpu.VMEM((SLOTS, 2, HEADS, BLOCK), F32),
            pltpu.VMEM(tile, F32),
            pltpu.VMEM(tile, F32),
            pltpu.VMEM((heads, 8, BLOCK), F32),
            dma,
            dma((4, HEADS)),
            dma((4, HEADS)),
            dma((CHUNKS, 6)),
            dma((CHUNKS, 6)),
            dma((CHUNKS, 6)),
            dma((CHUNKS, 6)),
            dma((CHUNKS, 6)),
            dma((CHUNKS, 6)),
            dma((6, 2)),
            dma((6, 2)),
            dma((heads - 1,)),
            dma((heads - 1,)),
        ],
        compiler_params=pltpu.CompilerParams(
            collective_id=0, has_side_effects=True, vmem_limit_bytes=VMEM
        ),
        cost_estimate=pl.CostEstimate(
            flops=2_000_000_000, bytes_accessed=2 * 1024 * 1024, transcendentals=2_000_000
        ),
    )(queries, keys, values, pattern.T, upstream)
    return pl.pallas_call(
        copy_kernel,
        out_shape=(out,) * 4,
        in_specs=[anywhere] * 4,
        out_specs=[anywhere] * 4,
        scratch_shapes=[pltpu.VMEM((4, tokens, width), BF16), dma((2, 4, 2))],
        compiler_params=pltpu.CompilerParams(vmem_limit_bytes=VMEM),
    )(*results)


def solution(mesh):
    return jax.shard_map(
        shards,
        mesh=mesh,
        in_specs=(P("ctx", "head"), P("ctx", "head"), P("ctx", "head"), P(), P("ctx", "head")),
        out_specs=(P("ctx", "head"), P("ctx", "head"), P("ctx", "head"), P("ctx", "head")),
        check_vma=False,
    )
```

```python
import functools
import math

import jax
import jax.numpy as jnp
from jax import lax
from jax.experimental import pallas as pl
from jax.experimental.pallas import tpu as pltpu
from jax.sharding import PartitionSpec as P

HD = 128
BLOCK = 128
WIDTH = 4096
HEADS = 8
SLOTS = 7
OWN = 6
LEVELS = 7
BLOCKS = 64
CHUNKS = 4
VMEM = 63 * 1024 * 1024
PER = HEADS // CHUNKS
LEAD = 1
LAG_B = 1
LAG_C = 2
LAG_QA = 1
LAG_QB = 2
G_LAG_P = 1
KV_RELAYED = 0
Q_RELAYED = 4
G_RELAYED = 0
G_LAG_B = 1
G_LAG_C = 2
NEG_BIG = -1e30
EPSILON = 1e-06
SCALE = HD**-0.5
SCALE2 = SCALE * math.log2(math.e)
MESH = pl.DeviceIdType.MESH
F32 = jnp.float32
BF16 = jnp.bfloat16


def nt(a, b):
    return lax.dot_general(a, b, (((1,), (1,)), ((), ())), preferred_element_type=F32)


def nn(a, b):
    return lax.dot_general(a, b, (((1,), (0,)), ((), ())), preferred_element_type=F32)


class Flow:
    def __init__(self, buf, send_sem, recv_sem, place, head, mirrored, relayed):
        self.buf, self.send_sem, self.recv_sem = buf, send_sem, recv_sem
        self.mirrored, self.head, self.relayed = mirrored, head, relayed
        self.j = BLOCKS - 1 - place if mirrored else place
        self.z, self.x, self.c = self.j // 8, (self.j // 2) % 4, self.j % 2

    def to(self, z, x, c):
        index = z * 8 + x * 2 + c
        index = BLOCKS - 1 - index if self.mirrored else index
        return (lax.rem(index + BLOCKS, BLOCKS), self.head)

    def copy(self, g, source, k, target=None):
        rows = pl.ds(g * PER, PER)
        return pltpu.make_async_remote_copy(
            src_ref=self.buf.at[rows, source],
            dst_ref=self.buf.at[rows, k],
            send_sem=self.send_sem.at[g, k],
            recv_sem=self.recv_sem.at[g, k],
            device_id=target or self.to(self.z, self.x, 1 - self.c),
            device_id_type=MESH,
        )

    def send(self, condition, g, source, k, z, x, c):
        @pl.when(condition)
        def _():
            self.copy(g, source, k, self.to(z, x, c)).start()

    def own(self, g):
        z, x, c = self.z, self.x, self.c
        self.send(z < 7, g, OWN, 3, z + 1, x, c)

    def own_x(self, g):
        z, x, c = self.z, self.x, self.c
        self.send(x < 3, g, OWN, 1, z, x + 1, c)
        self.send(x < 2, g, OWN, 2, z, x + 2, c)
        self.send(c == 0, g, OWN, 0, z, x, 1)

    def direct(self, g):
        return ((self.z == 1) | (self.z == 3)) & (g >= self.relayed)

    def relay(self, g):
        z = self.z
        return (z == 2) | (z == 4) | (((z == 3) | (z == 5)) & (g < self.relayed))

    def far(self, g):
        self.send(self.direct(g), g, OWN, 5, self.z + 4, self.x, self.c)

    def stage_a(self, g):
        z, x, c = self.z, self.x, self.c

        @pl.when(z >= 1)
        def _():
            self.copy(g, OWN, 3).wait_recv()
            self.send(z < 7, g, 3, 4, z + 1, x, c)
            self.send(x == 3, g, 3, 1, z, 0, c)
            self.send(x >= 2, g, 3, 2, z, x - 2, c)

    def stage_b(self, g):
        z, x, c = self.z, self.x, self.c

        @pl.when(z >= 2)
        def _():
            self.copy(g, OWN, 4).wait_recv()
            self.send(self.relay(g), g, 4, 5, z + 2, x, c)

        @pl.when(self.j >= 2)
        def _():
            self.copy(g, OWN, 1).wait_recv()
            self.send(c == 1, g, 1, 0, z, x, 0)

    def stage_c(self, g):
        for condition, k in ((self.j >= 1, 0), (self.j >= 4, 2), (self.z >= 4, 5)):

            @pl.when(condition)
            def _():
                self.copy(g, OWN, k).wait_recv()

    def drain(self, g):
        z, x, c, j = self.z, self.x, self.c, self.j
        for condition, k in (
            ((c == 0) | (j >= 2), 0),
            ((x < 3) | (z >= 1), 1),
            ((x < 2) | (z >= 1), 2),
            (z < 7, 3),
            ((z >= 1) & (z < 7), 4),
            (self.direct(g) | self.relay(g), 5),
        ):

            @pl.when(condition)
            def _():
                self.copy(g, OWN, k).wait_send()

    def clear(self):
        for k in range(6):

            @pl.when(self.j < 2**k)
            def _():
                self.buf[:, k] = jnp.zeros(self.buf.shape[:1] + self.buf.shape[2:], self.buf.dtype)


def kernel(
    q_ref,
    k_ref,
    v_ref,
    pattern_hbm,
    u_ref,
    normed_ref,
    dq_ref,
    dk_ref,
    dv_ref,
    pattern_ref,
    staged,
    kv,
    qs,
    gs,
    up,
    attn,
    probs,
    probs_t,
    row_scale,
    delta,
    stat_tile,
    stats,
    squares,
    crosses,
    y_buf,
    pattern_sem,
    load_sem,
    store_sem,
    kv_send,
    kv_recv,
    q_send,
    q_recv,
    g_send,
    g_recv,
    stat_send,
    stat_recv,
    y_send,
    y_recv,
):
    place = lax.axis_index("ctx")
    head = lax.axis_index("head")
    heads = lax.axis_size("head")
    z, x, c = place // 8, (place // 2) % 4, place % 2

    barrier = pltpu.get_barrier_semaphore()

    def ring(dz, dx, dc):
        return ((z + dz) % 8) * 8 + ((x + dx) % 4) * 2 + (c + dc) % 2

    partners = [(ring(d, 0, 0), head) for d in (1, 2, 4, 6, 7)]
    partners += [(ring(0, d, 0), head) for d in (1, 2, 3)]
    partners += [(ring(0, 0, 1), head)]
    partners += [((place + d) % BLOCKS, head) for d in (1, 2, 4, 60, 62, 63)]
    partners += [(place, (head + d) % heads) for d in range(1, heads)]
    for partner in partners:
        pl.semaphore_signal(barrier, inc=1, device_id=partner, device_id_type=MESH)

    loads = [pltpu.make_async_copy(pattern_hbm, pattern_ref, pattern_sem)]
    for h in range(HEADS):
        columns = pl.ds(h * HD, HD)
        for a, (ref, target) in enumerate(
            (
                (k_ref, kv.at[h, OWN, 0]),
                (v_ref, kv.at[h, OWN, 1]),
                (q_ref, qs.at[h, OWN]),
                (u_ref, up.at[h]),
            )
        ):
            copy = pltpu.make_async_copy(ref.at[:, columns], target, load_sem.at[a, h])
            loads.append(copy)
    for copy in loads:
        copy.start()

    kv_flow = Flow(kv, kv_send, kv_recv, place, head, False, KV_RELAYED)
    q_flow = Flow(qs, q_send, q_recv, place, head, True, Q_RELAYED)
    g_flow = Flow(gs, g_send, g_recv, place, head, True, G_RELAYED)
    for flow in (kv_flow, q_flow, g_flow):
        flow.clear()
    for k in range(6):

        @pl.when(g_flow.j < 2**k)
        def _():
            stats[k] = jnp.zeros(stats.shape[1:], F32)

    squares[...] = jnp.zeros(squares.shape, F32)
    crosses[...] = jnp.zeros(crosses.shape, F32)
    stat_tile[...] = jnp.zeros(stat_tile.shape, F32)
    first = [copy for i, copy in enumerate(loads[1:]) if i % 4 < 2]
    rest = loads[:1] + [copy for i, copy in enumerate(loads[1:]) if i % 4 >= 2]
    for copy in first:
        copy.wait()
    pl.semaphore_wait(barrier, len(partners))

    def every(body, count=CHUNKS):
        def step(g, carry):
            body(g)
            return carry

        lax.fori_loop(0, count, step, 0)

    def kv_send_chunk(g):
        kv_flow.own(g)
        kv_flow.far(g)

    every(kv_send_chunk, LEAD)
    for copy in rest:
        copy.wait()

    row = lax.broadcasted_iota(jnp.int32, (BLOCK, BLOCK), 0)
    lane = lax.broadcasted_iota(jnp.int32, (BLOCK, BLOCK), 1)

    def bias_of(index, k):
        return jnp.where(pattern_ref[k, index] >= 0, 0.0, NEG_BIG).astype(F32)

    def slot(array, s):
        return array[:, s * BLOCK : (s + 1) * BLOCK]

    results = (normed_ref, dq_ref, dk_ref, dv_ref)

    def store(a, h):
        columns = pl.ds(pl.multiple_of(h * HD, HD), HD)
        return pltpu.make_async_copy(
            staged.at[a, h], results[a].at[:, columns], store_sem.at[a, h]
        )

    def put(a, h, value):
        staged[a, h] = value
        store(a, h).start()

    def forward(h):
        raw = nt(qs[h, OWN], kv[h, :, 0].reshape(SLOTS * BLOCK, HD))
        scores = [slot(raw, s) * SCALE2 + bias_of(place, s) for s in range(OWN)]
        scores.append(jnp.where(lane <= row, slot(raw, OWN) * SCALE2, NEG_BIG))
        highest = jnp.max(functools.reduce(jnp.maximum, scores), axis=1, keepdims=True)
        weights = [jnp.exp2(s - highest) for s in scores]
        total = jnp.sum(functools.reduce(jnp.add, weights), axis=1, keepdims=True)
        inverse_total = 1.0 / total
        rounded = jnp.concatenate([w.astype(BF16) for w in weights], axis=1)
        probs[h] = rounded
        out = nn(rounded, kv[h, :, 1].reshape(SLOTS * BLOCK, HD)) * inverse_total
        out = out.astype(BF16)
        attn[h] = out
        wide = out.astype(F32)
        squares[...] += wide * wide
        crosses[...] += wide * up[h].astype(F32)
        row_scale[h] = inverse_total * SCALE
        stat_tile[...] = jnp.where(lane == h, highest + jnp.log2(total), stat_tile[...])

    def heads_of(g, body):
        def step(i, carry):
            body(g * PER + i)
            return carry

        lax.fori_loop(0, PER, step, 0)

    def at(step, body):
        @pl.when((step >= 0) & (step < CHUNKS))
        def _():
            body(step)

    def kv_done(g):
        kv_flow.stage_c(g)
        heads_of(g, forward)

    def q_send_chunk(g):
        q_flow.own(g)
        q_flow.far(g)

    def first_phase(s):
        at(s, kv_flow.stage_a)

        @pl.when(s < CHUNKS - LEAD)
        def _():
            kv_send_chunk(s + LEAD)

        at(s, kv_flow.own_x)

        at(s - LAG_B, kv_flow.stage_b)
        at(s, q_send_chunk)
        at(s, q_flow.own_x)
        at(s - LAG_QA, q_flow.stage_a)
        at(s - LAG_QB, q_flow.stage_b)
        at(s - LAG_C, kv_done)

    every(first_phase, CHUNKS + max(LAG_C, LAG_QB))

    stats[OWN, 0] = stat_tile[...].T[:HEADS]

    def stat_copy(k, part):
        return pltpu.make_async_remote_copy(
            src_ref=stats.at[OWN, part],
            dst_ref=stats.at[k, part],
            send_sem=stat_send.at[k, part],
            recv_sem=stat_recv.at[k, part],
            device_id=(lax.rem(place - 2**k + BLOCKS, BLOCKS), head),
            device_id_type=MESH,
        )

    def stat_start(part):
        for k in range(6):

            @pl.when(place >= 2**k)
            def _():
                stat_copy(k, part).start()

    def stat_wait(part):
        for k in range(6):

            @pl.when(place + 2**k < BLOCKS)
            def _():
                stat_copy(k, part).wait_recv()

    square = jnp.sum(squares[...], axis=1, keepdims=True)
    cross = jnp.sum(crosses[...], axis=1, keepdims=True)
    tile = jnp.where(lane == 0, square, jnp.where(lane == 1, cross, 0.0))
    y_buf[heads - 1] = tile.T[:8]
    copies = []
    for d in range(1, heads):
        copy = pltpu.make_async_remote_copy(
            src_ref=y_buf.at[heads - 1],
            dst_ref=y_buf.at[d - 1],
            send_sem=y_send.at[d - 1],
            recv_sem=y_recv.at[d - 1],
            device_id=(place, (head + d) % heads),
            device_id_type=MESH,
        )
        copy.start()
        copies.append(copy)
    stat_start(0)

    for copy in copies:
        copy.wait_recv()
    sums = functools.reduce(jnp.add, [y_buf[d] for d in range(heads)])
    sums = jnp.concatenate([sums, jnp.zeros((BLOCK - 8, BLOCK), F32)], axis=0).T
    inverse = lax.rsqrt(sums[:, 0:1] / WIDTH + EPSILON)
    factor = inverse * inverse * inverse * sums[:, 1:2] / WIDTH

    def gradient(h):
        wide = attn[h].astype(F32)
        grad = (inverse * up[h].astype(F32) - wide * factor).astype(BF16)
        gs[h, OWN] = grad
        put(0, h, (wide * inverse).astype(BF16))
        here = jnp.sum(grad.astype(F32) * wide, axis=1, keepdims=True)
        delta[h] = here
        stat_tile[...] = jnp.where(lane == h, here, stat_tile[...])

    def g_send(g):
        g_flow.own(g)
        g_flow.own_x(g)
        g_flow.far(g)

    def gradient_chunk(g):
        heads_of(g, gradient)

    every(gradient_chunk)
    stats[OWN, 1] = stat_tile[...].T[:HEADS]
    stat_start(1)

    def grad_query(h):
        grad_probs = nt(gs[h, OWN], kv[h, :, 1].reshape(SLOTS * BLOCK, HD))
        held = probs[h].astype(F32)
        dscore = (held * (grad_probs - delta[h]) * row_scale[h]).astype(BF16)
        put(1, h, nn(dscore, kv[h, :, 0].reshape(SLOTS * BLOCK, HD)).astype(BF16))

    def key_probs(h):
        raw = nt(kv[h, OWN, 0], qs[h].reshape(SLOTS * BLOCK, HD))
        parts = []
        for s in range(SLOTS):
            scores = slot(raw, s) * SCALE2 - stats[s, 0, pl.ds(h, 1), :]
            if s == OWN:
                scores = jnp.where(row <= lane, scores, NEG_BIG)
            else:
                index = place + 2**s
                live = (pattern_ref[s, jnp.minimum(index, BLOCKS - 1)] >= 0) & (index < BLOCKS)
                scores = scores + jnp.where(live, 0.0, NEG_BIG).astype(F32)
            parts.append(jnp.exp2(scores).astype(BF16))
        probs_t[h] = jnp.concatenate(parts, axis=1)

    def grad_keys(h):
        grads = gs[h].reshape(SLOTS * BLOCK, HD)
        held = probs_t[h]
        put(3, h, nn(held, grads).astype(BF16))
        raw = nt(kv[h, OWN, 1], grads)
        parts = []
        for s in range(SLOTS):
            part = slot(raw, s) - stats[s, 1, pl.ds(h, 1), :]
            parts.append((slot(held, s).astype(F32) * part * SCALE).astype(BF16))
        dscore = jnp.concatenate(parts, axis=1)
        put(2, h, nn(dscore, qs[h].reshape(SLOTS * BLOCK, HD)).astype(BF16))

    every(g_send)

    def key_probs_chunk(g):
        @pl.when(g == 0)
        def _():
            stat_wait(0)

        q_flow.stage_c(g)
        heads_of(g, key_probs)

    def key_grads(g):
        @pl.when(g == 0)
        def _():
            stat_wait(1)

        g_flow.stage_c(g)
        heads_of(g, grad_keys)

    def grad_query_chunk(g):
        heads_of(g, grad_query)

    def second_phase(s):
        at(s, grad_query_chunk)
        at(s, g_flow.stage_a)
        at(s - G_LAG_B, g_flow.stage_b)
        at(s - G_LAG_P, key_probs_chunk)
        at(s - G_LAG_C, key_grads)

    every(second_phase, CHUNKS + G_LAG_C)

    every(kv_flow.drain)
    every(q_flow.drain)
    every(g_flow.drain)
    for copy in copies:
        copy.wait_send()
    for k in range(6):

        @pl.when(place >= 2**k)
        def _():
            stat_copy(k, 0).wait_send()
            stat_copy(k, 1).wait_send()

    def stored(h):
        for a in range(4):
            store(a, h).wait()

    every(stored, HEADS)


def copy_kernel(*refs):
    sources, targets, held, sem = refs[:4], refs[4:8], refs[8], refs[9]
    pieces = []
    for a in range(4):
        for part in range(4):
            rows = pl.ds(part * BLOCK // 4, BLOCK // 4)
            here = held.at[a, rows]
            pieces.append(
                (
                    pltpu.make_async_copy(sources[a].at[rows], here, sem.at[0, a, part]),
                    pltpu.make_async_copy(here, targets[a].at[rows], sem.at[1, a, part]),
                )
            )
    for load, _ in pieces:
        load.start()
    for load, store in pieces:
        load.wait()
        store.start()
    for _, store in pieces:
        store.wait()


def shards(queries, keys, values, pattern, upstream):
    heads = lax.axis_size("head")
    tokens, width = queries.shape
    out = jax.ShapeDtypeStruct((tokens, width), BF16)
    tile = (BLOCK, HD)
    dma = pltpu.SemaphoreType.DMA
    anywhere = pl.BlockSpec(memory_space=pl.ANY)
    results = pl.pallas_call(
        kernel,
        out_shape=(out,) * 4,
        in_specs=[
            anywhere,
            anywhere,
            anywhere,
            anywhere,
            anywhere,
        ],
        out_specs=[anywhere] * 4,
        scratch_shapes=[
            pltpu.SMEM((LEVELS + 1, BLOCKS), jnp.int32),
            pltpu.VMEM((4, HEADS) + tile, BF16),
            pltpu.VMEM((HEADS, SLOTS, 2) + tile, BF16),
            pltpu.VMEM((HEADS, SLOTS) + tile, BF16),
            pltpu.VMEM((HEADS, SLOTS) + tile, BF16),
            pltpu.VMEM((HEADS,) + tile, BF16),
            pltpu.VMEM((HEADS,) + tile, BF16),
            pltpu.VMEM((HEADS, BLOCK, SLOTS * BLOCK), BF16),
            pltpu.VMEM((HEADS, BLOCK, SLOTS * BLOCK), BF16),
            pltpu.VMEM((HEADS, BLOCK, 1), F32),
            pltpu.VMEM((HEADS, BLOCK, 1), F32),
            pltpu.VMEM((BLOCK, BLOCK), F32),
            pltpu.VMEM((SLOTS, 2, HEADS, BLOCK), F32),
            pltpu.VMEM(tile, F32),
            pltpu.VMEM(tile, F32),
            pltpu.VMEM((heads, 8, BLOCK), F32),
            dma,
            dma((4, HEADS)),
            dma((4, HEADS)),
            dma((CHUNKS, 6)),
            dma((CHUNKS, 6)),
            dma((CHUNKS, 6)),
            dma((CHUNKS, 6)),
            dma((CHUNKS, 6)),
            dma((CHUNKS, 6)),
            dma((6, 2)),
            dma((6, 2)),
            dma((heads - 1,)),
            dma((heads - 1,)),
        ],
        compiler_params=pltpu.CompilerParams(
            collective_id=0, has_side_effects=True, vmem_limit_bytes=VMEM
        ),
        cost_estimate=pl.CostEstimate(
            flops=2_000_000_000, bytes_accessed=2 * 1024 * 1024, transcendentals=2_000_000
        ),
    )(queries, keys, values, pattern.T, upstream)
    return pl.pallas_call(
        copy_kernel,
        out_shape=(out,) * 4,
        in_specs=[anywhere] * 4,
        out_specs=[anywhere] * 4,
        scratch_shapes=[pltpu.VMEM((4, tokens, width), BF16), dma((2, 4, 4))],
        compiler_params=pltpu.CompilerParams(vmem_limit_bytes=VMEM),
    )(*results)


def solution(mesh):
    return jax.shard_map(
        shards,
        mesh=mesh,
        in_specs=(P("ctx", "head"), P("ctx", "head"), P("ctx", "head"), P(), P("ctx", "head")),
        out_specs=(P("ctx", "head"), P("ctx", "head"), P("ctx", "head"), P("ctx", "head")),
        check_vma=False,
    )
```
